32 devices in a mesh: seq: 8 (over z, x), ch: 4 (over y, core).
Axes of the slice: x: 2, y: 2, z: 4, core: 2. Of those that a mesh axis runs over, the one named last changes fastest.
Arguments:
- features: bfloat16 [4096, 1024], P('seq', 'ch'), may hold values from -6 to 6
- w_qkv: bfloat16 [1024, 3072], P('ch'), may hold values from -0.1875 to 0.1875
- log_gate: float32 [8, 4096], P(None, ('seq', 'ch')), may hold values from -1 to 0
- norm_gain: float32 [1024], replicated, may hold values from 0.1 to 1.9
- w_pred: bfloat16 [4, 1024, 1024], replicated, may hold values from -0.1875 to 0.1875
- patch_mask: int32 [4096], P(('seq', 'ch')), may hold values 0 or 1
- neg_index: int32 [4, 32], P(None, ('seq', 'ch')), may hold values from 0 to 4095, as said below
Outputs:
- context: bfloat16 [4096, 1024], P(('seq', 'ch'))
- nce_loss: float32 [4, 4096], P(None, ('seq', 'ch'))
The draws below stay inside these ranges and needn't reach their ends.
Inputs may be any that keep to these rules, and one draw needn't show every extreme that they name: `neg_index`: negative n of every offset lies among the 128 patches of block n, blocks of 128 consecutive patches.
All inputs are finite; a program needn't handle non-finite values. No bound on the sum of `patch_mask` on one device may be relied on, other than what follows from the above.
Results may differ from the reference program's by a relative error of at most 0.0061.
Values may be sent and summed in bfloat16 or wider, within the bound.
A program may use at most 320 MiB of HBM per device.

```python
import math
import jax
import jax.numpy as jnp
from jax import lax

CIN = 1024
HEADS = 8
HEAD_DIM = 128
K = 4
TOK_DEV = 128
NEG_DEV = 1
HD = 1024
ROW_W = 64
SLIDE_PATCHES = 4096
NNEG = 32


def draw_log_gate(key, part):
    portion_count = jax.random.split(key, 8)
    fast_count = jax.random.randint(portion_count[0], (), 1, HEADS)
    order = jax.random.permutation(portion_count[1], HEADS)
    fast = (order < fast_count).astype(jnp.float32)
    fast_rate = jnp.exp(jax.random.uniform(portion_count[2], (HEADS,), jnp.float32, math.log(1.0 / 50.0), math.log(1.0 / 30.0)))
    slow_rate = jnp.exp(jax.random.uniform(portion_count[3], (HEADS,), jnp.float32, math.log(0.02), math.log(0.25))) * (math.log(10.0) / SLIDE_PATCHES)
    arrival_rate = fast * fast_rate + (1.0 - fast) * slow_rate
    token_multiplier = jax.random.uniform(portion_count[4], (HEADS, SLIDE_PATCHES), jnp.float32, 0.5, 1.5)
    block_multiplier = jnp.exp(jax.random.uniform(portion_count[5], (HEADS, SLIDE_PATCHES // TOK_DEV, 1), jnp.float32, math.log(0.5), math.log(2.0)))
    block_multiplier = jnp.broadcast_to(block_multiplier, (HEADS, SLIDE_PATCHES // TOK_DEV, TOK_DEV)).reshape(HEADS, SLIDE_PATCHES)
    spike_position = jax.random.randint(portion_count[6], (3,), 0, SLIDE_PATCHES)
    spike_length = jnp.log(jax.random.uniform(portion_count[7], (3, 1), jnp.float32, 0.5, 0.8))
    match_count = jnp.arange(SLIDE_PATCHES)[None, :] == spike_position[:, None]
    spike_event = jnp.sum(jnp.where(match_count, spike_length, 0.0), axis=0)
    return -arrival_rate[:, None] * token_multiplier * block_multiplier + spike_event[None, :]


def draw_neg_index(key, part):
    offsets = jax.random.randint(key, (K, NNEG), 0, TOK_DEV)
    column = jnp.arange(NNEG)[None, :]
    row = jnp.arange(K)[:, None]
    chosen = column // NEG_DEV * TOK_DEV + offsets
    first = (row == 0) & (column == 0)
    last = (row == 0) & (column == NNEG - 1)
    chosen = jnp.where(first, 0, chosen)
    chosen = jnp.where(last, SLIDE_PATCHES - 1, chosen)
    return chosen.astype(jnp.int32)


def plant(drawn, key, least, top_value):
    index_at = [jax.random.randint(jax.random.fold_in(key, axis), (), 0, length) for axis, length in enumerate(drawn.shape)]
    longest = drawn.shape.index(max(drawn.shape))
    neighbour = index_at[:longest] + [(index_at[longest] + 1) % drawn.shape[longest]] + index_at[longest + 1:]
    return drawn.at[tuple(index_at)].set(least).at[tuple(neighbour)].set(top_value)


def block_levels(rng, dims, cuts, smallest, largest):
    def one(dim, blocks):
        draws = jax.random.uniform(jax.random.fold_in(jax.random.fold_in(rng, 6), dim), (blocks,), jnp.float32, smallest / len(cuts), largest / len(cuts))
        return jnp.repeat(jnp.exp(draws), dims[dim] // blocks).reshape((-1,) + (1,) * (len(dims) - dim - 1))

    level = one(*cuts[0])
    for cut in cuts[1:]:
        level = level * one(*cut)
    return level


def noise(rng, dims, width, most, pieces=(), held_as=jnp.bfloat16):
    result = width * jax.random.normal(rng, dims, jnp.float32)
    if pieces:
        result = result * block_levels(rng, dims, pieces, -0.22, 0.18)
    return jnp.clip(result, -most, most).astype(held_as)


def setup_inputs(seed: int = 0) -> dict:
    seeds = jax.random.split(jax.random.key(seed), 8)
    return {
        "features": noise(seeds[0], (SLIDE_PATCHES, CIN), 1.0, 6.0, ((0, 8), (1, 4))),
        "w_qkv": noise(seeds[1], (CIN, 3 * HD), CIN ** -0.5, 0.1875, ((0, 4),)),
        "log_gate": draw_log_gate(jax.random.fold_in(seeds[7], 71), 0),
        "norm_gain": jnp.clip(1.0 + 0.18 * jax.random.normal(seeds[3], (HD,), jnp.float32), 0.1, 1.9),
        "w_pred": noise(seeds[4], (K, HD, CIN), HD ** -0.5, 0.1875),
        "patch_mask": plant((jax.random.randint(seeds[5], (SLIDE_PATCHES,), 0, 8) < 7).astype(jnp.int32), jax.random.fold_in(seeds[5], 1), 0, 1),
        "neg_index": draw_neg_index(jax.random.fold_in(seeds[7], 71), 0),
    }


def reference(features, w_qkv, log_gate, norm_gain, w_pred, patch_mask, neg_index):
    inner = HEADS * HEAD_DIM
    highest = lax.Precision.HIGHEST
    score_scale = 4.0 * CIN ** (-0.5)
    projected = jnp.dot(features, w_qkv, preferred_element_type=jnp.float32).astype(jnp.bfloat16)
    mask_wire = patch_mask.astype(jnp.bfloat16)
    queries = projected[:, :inner].astype(jnp.float32)
    keys_all = projected[:, inner:2 * inner].astype(jnp.float32)
    values = (projected[:, 2 * inner:] * mask_wire[:, None]).astype(jnp.float32)
    blocks = SLIDE_PATCHES // TOK_DEV
    q_blocks = queries.reshape(blocks, TOK_DEV, HEADS, HEAD_DIM)
    k_blocks = keys_all.reshape(blocks, TOK_DEV, HEADS, HEAD_DIM)
    v_blocks = values.reshape(blocks, TOK_DEV, HEADS, HEAD_DIM)
    g_blocks = jnp.transpose(log_gate.reshape(HEADS, blocks, TOK_DEV), (1, 0, 2))
    lower = jnp.arange(TOK_DEV)[:, None] >= jnp.arange(TOK_DEV)[None, :]

    def step(state, inputs):
        q_part, k_part, v_part, g_part = inputs
        cumul = jnp.cumsum(g_part, axis=1)
        scores = jnp.einsum('thd,shd->hts', q_part, k_part, precision=highest)
        diff = cumul[:, :, None] - cumul[:, None, :]
        decay = jnp.where(lower[None], jnp.exp(jnp.where(lower[None], diff, 0.0)), 0.0)
        intra = jnp.einsum('hts,shd->thd', scores * decay, v_part, precision=highest)
        inter = jnp.einsum('thd,hde->the', q_part, state, precision=highest) * jnp.exp(cumul).T[:, :, None]
        tail = jnp.exp(cumul[:, -1:] - cumul)
        summary = jnp.einsum('shd,she->hde', k_part * tail.T[:, :, None], v_part, precision=highest)
        new_state = jnp.exp(cumul[:, -1])[:, None, None] * state + summary
        return (new_state, (intra + inter) * HEAD_DIM ** (-0.5))
    start_state = jnp.zeros((HEADS, HEAD_DIM, HEAD_DIM), jnp.float32)
    _, mixed = lax.scan(step, start_state, (q_blocks, k_blocks, v_blocks, g_blocks))
    mixed = mixed.reshape(SLIDE_PATCHES, HEADS, HEAD_DIM)
    squares = lax.optimization_barrier(jnp.mean(mixed * mixed, axis=-1, keepdims=True))
    normed = (mixed / jnp.sqrt(squares + 1e-06)).reshape(SLIDE_PATCHES, inner)
    context = (normed * norm_gain).astype(jnp.bfloat16)
    maskf = patch_mask.astype(jnp.float32)
    padded = jnp.concatenate([features, jnp.zeros((K * ROW_W, CIN), jnp.bfloat16)], axis=0)
    mask_pad = jnp.concatenate([maskf, jnp.zeros((K * ROW_W,), jnp.float32)], axis=0)
    losses = []
    for offset in range(K):
        predicted = jnp.dot(context, w_pred[offset], preferred_element_type=jnp.float32).astype(jnp.bfloat16)
        shift_rows = (offset + 1) * ROW_W
        target = lax.dynamic_slice_in_dim(padded, shift_rows, SLIDE_PATCHES, 0)
        target_mask = lax.dynamic_slice_in_dim(mask_pad, shift_rows, SLIDE_PATCHES, 0)
        positive = jnp.einsum('tc,tc->t', predicted.astype(jnp.float32), target.astype(jnp.float32)) * score_scale
        bank = jnp.take(features, neg_index[offset], axis=0)
        logits = jnp.dot(predicted, bank.T, preferred_element_type=jnp.float32) * score_scale
        negsum = lax.optimization_barrier(jnp.sum(jnp.exp(logits), axis=1))
        valid = maskf * target_mask
        losses.append(valid * (jnp.log(jnp.exp(positive) + negsum) - positive))
    return (context, jnp.stack(losses, axis=0))
```

```python
import functools

import jax
import jax.numpy as jnp
from jax import lax
from jax.experimental import pallas as pl
from jax.experimental.pallas import tpu as pltpu
from jax.sharding import PartitionSpec as P

HEADS = 8
HEAD_DIM = 128
K = 4
MASK_ROW = 8
NEG_ROW = 9
AUX_ROWS = 16
MESH = pl.DeviceIdType.MESH
norm_eps = 1e-06
highest = lax.Precision.HIGHEST
across = (((1,), (1,)), ((), ()))
down = (((0,), (0,)), ((), ()))


def dot(a, b, dims=(((1,), (0,)), ((), ())), precision=None):
    return lax.dot_general(a, b, dims, precision=precision, preferred_element_type=jnp.float32)


def split(x):
    high = x.astype(jnp.bfloat16)
    return high, (x - high.astype(jnp.float32)).astype(jnp.bfloat16)


def kernel(
    S, C,
    feat_hbm, w_hbm, gate_ref, gain_ref, wpred_hbm, mask_ref, neg_ref,
    ctx_ref, loss_ref,
    feat_all, w_all, aux_all, sel, totals, bank, proj, qkv, cumrow, cumcol,
    state_out, state_in, carried, ctx_out, ctx_in, wpred,
    local_sem, ch_send, ch_recv, tot_send, tot_recv, bank_send, bank_recv,
    ext_send, ext_recv, st_send, st_recv, ctx_send, ctx_recv,
):
    L = gate_ref.shape[1]
    B = C * L
    CB = feat_hbm.shape[1]
    W = qkv.shape[2]
    inner = HEADS * HEAD_DIM
    own_heads = W // HEAD_DIM
    row_width = L // 2
    score_scale = 4.0 * (C * CB) ** (-0.5)
    s, c = lax.axis_index("seq"), lax.axis_index("ch")

    own = [pltpu.make_async_copy(feat_hbm, feat_all.at[c, pl.ds(0, B)], local_sem.at[0])]
    for p in range(3):
        begin = pl.multiple_of(p * inner + c * W, 128)
        own.append(
            pltpu.make_async_copy(w_hbm.at[:, pl.ds(begin, W)], w_all.at[c, p], local_sem.at[1 + p])
        )
    own.append(pltpu.make_async_copy(wpred_hbm, wpred, local_sem.at[4]))
    for copy in own:
        copy.start()

    aux_all[c, 0:HEADS] = gate_ref[...]
    base = (s * C + c) * L
    local_index = (neg_ref[...] - base).astype(jnp.float32)
    lead = jnp.where(
        lax.broadcasted_iota(jnp.int32, (HEADS, L), 0) == 0,
        jnp.broadcast_to(mask_ref[...].astype(jnp.float32), (HEADS, L)),
        0.0,
    )
    aux_all[c, HEADS:AUX_ROWS] = lead
    aux_all[c, NEG_ROW : NEG_ROW + K] = jnp.broadcast_to(local_index, (K, L))

    barrier = pltpu.get_barrier_semaphore()
    for d in range(1, C):
        pl.semaphore_signal(
            barrier, inc=1, device_id=(s, lax.rem(c + d, C)), device_id_type=MESH
        )
    for d in range(1, S):
        pl.semaphore_signal(
            barrier, inc=1, device_id=(lax.rem(s + d, S), c), device_id_type=MESH
        )
    pl.semaphore_wait(barrier, S + C - 2)

    def to_ch(d, kind):
        peer = lax.rem(c + d, C)
        if kind == 0:
            source, target = aux_all.at[c], aux_all.at[c]
        elif kind == 1:
            source, target = feat_hbm, feat_all.at[c, pl.ds(0, B)]
        else:
            begin = pl.multiple_of((kind - 2) * inner + peer * W, 128)
            source, target = w_hbm.at[:, pl.ds(begin, W)], w_all.at[c, kind - 2]
        return pltpu.make_async_remote_copy(
            source, target, ch_send.at[d - 1, kind], ch_recv.at[d - 1, kind],
            device_id=(s, peer), device_id_type=MESH,
        )

    def to_seq(source, target, sends, recvs, d):
        return pltpu.make_async_remote_copy(
            source, target, sends.at[d - 1], recvs.at[d - 1],
            device_id=(lax.rem(s + d, S), c), device_id_type=MESH,
        )

    sent = [to_ch(d, kind) for kind in range(5) for d in range(1, C)]
    for copy in sent:
        copy.start()
    for d in range(1, C):
        to_ch(d, 0).wait_recv()

    row_id = lax.broadcasted_iota(jnp.int32, (L, L), 0)
    column_id = lax.broadcasted_iota(jnp.int32, (L, L), 1)
    lower = row_id >= column_id
    tril = lower.astype(jnp.float32)
    triu = (row_id <= column_id).astype(jnp.float32)
    sel[...] = jnp.zeros_like(sel)
    row_carry = jnp.zeros((8, 1), jnp.float32)
    column_carry = jnp.zeros((1, 8), jnp.float32)
    for b in range(C):
        for i in range(own_heads):
            sel[b, i : i + 1] = aux_all[b, pl.ds(c * own_heads + i, 1), :]
        gates = sel[b]
        by_row = dot(gates, triu, precision=highest) + row_carry
        by_column = dot(tril, gates, across, precision=highest) + column_carry
        cumrow[:, b * L : (b + 1) * L] = by_row
        cumcol[b * L : (b + 1) * L, :] = by_column
        row_carry = by_row[:, L - 1 : L]
        column_carry = by_column[L - 1 : L, :]
    totals[s] = jnp.broadcast_to(row_carry, (8, 128))
    tot_copies = [to_seq(totals.at[s], totals.at[s], tot_send, tot_recv, d) for d in range(1, S)]
    for copy in tot_copies:
        copy.start()

    own[0].wait()
    for d in range(1, C):
        to_ch(d, 1).wait_recv()

    wanted = jnp.concatenate([aux_all[b, NEG_ROW : NEG_ROW + K, :] for b in range(C)], axis=0)
    negatives = K * C
    owner = lax.broadcasted_iota(jnp.int32, (negatives, L), 0) // K
    lane = lax.broadcasted_iota(jnp.int32, (negatives, L), 1).astype(jnp.float32)
    hit = wanted == lane
    chosen = jnp.concatenate(
        [jnp.where(hit & (owner == b), 1.0, 0.0) for b in range(C)], axis=1
    ).astype(jnp.bfloat16)
    for b in range(C):
        bank[s, b] = dot(chosen, feat_all[b, 0:B, :]).astype(jnp.bfloat16)
    bank_copies = [to_seq(bank.at[s], bank.at[s], bank_send, bank_recv, d) for d in range(1, S)]
    for copy in bank_copies:
        copy.start()

    def ext(kind):
        if kind == 0:
            source, target = feat_all.at[:, pl.ds(0, 2 * L)], feat_all.at[:, pl.ds(B, 2 * L)]
        else:
            source, target = aux_all.at[pl.ds(0, 2)], aux_all.at[pl.ds(C, 2)]
        return pltpu.make_async_remote_copy(
            source, target, ext_send.at[kind], ext_recv.at[kind],
            device_id=(lax.rem(s + S - 1, S), c), device_id_type=MESH,
        )

    reaching = c >= C - 2

    @pl.when(reaching & (s > 0))
    def _():
        ext(0).start()
        ext(1).start()

    @pl.when(s == S - 1)
    def _():
        feat_all[:, B : B + 2 * L, :] = jnp.zeros((C, 2 * L, CB), jnp.bfloat16)
        aux_all[C : C + 2] = jnp.zeros((2, AUX_ROWS, 128), jnp.float32)

    for d in range(C):
        block = lax.rem(c + C - d, C)
        for p in range(3):
            if d == 0:
                own[1 + p].wait()
            else:
                to_ch(d, 2 + p).wait_recv()
            part = dot(feat_all[block, 0:B, :], w_all[block, p])
            if d == 0:
                proj[p] = part
            elif d < C - 1:
                proj[p] = proj[p] + part
            else:
                qkv[p] = (proj[p] + part).astype(jnp.bfloat16)
    eye = (row_id == column_id).astype(jnp.bfloat16)
    for b in range(C):
        keep = dot(eye, aux_all[b].astype(jnp.bfloat16), across)[:, MASK_ROW : MASK_ROW + 1]
        rows = slice(b * L, (b + 1) * L)
        qkv[2, rows, :] = (qkv[2, rows, :].astype(jnp.float32) * keep).astype(jnp.bfloat16)

    for i in range(own_heads):
        head = slice(i * HEAD_DIM, (i + 1) * HEAD_DIM)
        tail = jnp.exp(cumcol[B - 1 : B, i : i + 1] - cumcol[:, i : i + 1])
        high, low = split(qkv[1, :, head].astype(jnp.float32) * tail)
        values = qkv[2, :, head]
        state_out[head, :] = (dot(high, values, down) + dot(low, values, down)).astype(jnp.bfloat16)

    def state_copy(d):
        return to_seq(state_out, state_in.at[s], st_send, st_recv, d)

    for d in reversed(range(1, S)):
        @pl.when(s + d < S)
        def _(d=d):
            state_copy(d).start()

    for i in range(own_heads):
        head = slice(i * HEAD_DIM, (i + 1) * HEAD_DIM)
        for b in range(C):
            rows = slice(b * L, (b + 1) * L)
            width = (b + 1) * L
            scores = dot(qkv[0, rows, head], qkv[1, 0:width, head], across)
            diff = cumcol[rows, i : i + 1] - cumrow[i : i + 1, 0:width]
            seen = (
                lax.broadcasted_iota(jnp.int32, (L, width), 0) + b * L
                >= lax.broadcasted_iota(jnp.int32, (L, width), 1)
            )
            decay = jnp.where(seen, jnp.exp(jnp.where(seen, diff, 0.0)), 0.0)
            high, low = split(scores * decay)
            values = qkv[2, 0:width, head]
            proj[0, rows, head] = dot(high, values) + dot(low, values)

    for d in range(1, S):
        to_seq(totals.at[s], totals.at[s], tot_send, tot_recv, d).wait_recv()
    carried[...] = jnp.zeros_like(carried)

    def absorb(turn, _):
        far = s - turn
        pltpu.make_async_remote_copy(
            state_out, state_in.at[turn], st_send.at[far - 1], st_recv.at[far - 1],
            device_id=(lax.rem(s + 1, S), c), device_id_type=MESH,
        ).wait_recv()
        total = totals[turn]
        for i in range(own_heads):
            head = slice(i * HEAD_DIM, (i + 1) * HEAD_DIM)
            carried[head, :] = (
                jnp.exp(total[i : i + 1, :]) * carried[head, :]
                + state_in[turn, head, :].astype(jnp.float32)
            )
        return 0

    lax.fori_loop(0, s, absorb, 0)

    for i in range(own_heads):
        head = slice(i * HEAD_DIM, (i + 1) * HEAD_DIM)
        high, low = split(carried[head, :])
        gain = gain_ref[pl.ds(c * own_heads + i, 1), :]
        for b in range(C):
            rows = slice(b * L, (b + 1) * L)
            queries = qkv[0, rows, head]
            inter = (dot(queries, high) + dot(queries, low)) * jnp.exp(cumcol[rows, i : i + 1])
            mixed = (proj[0, rows, head] + inter) * HEAD_DIM ** (-0.5)
            squares = jnp.mean(mixed * mixed, axis=-1, keepdims=True)
            normed = mixed / jnp.sqrt(squares + norm_eps)
            ctx_out[b, :, head] = (normed * gain).astype(jnp.bfloat16)

    def to_owner(d):
        peer = lax.rem(c + d, C)
        return pltpu.make_async_remote_copy(
            ctx_out.at[peer], ctx_in.at[c], ctx_send.at[d - 1], ctx_recv.at[d - 1],
            device_id=(s, peer), device_id_type=MESH,
        )

    for d in range(1, C):
        to_owner(d).start()
    ctx_in[c] = ctx_out[c]
    own[4].wait()
    for d in range(1, S):
        to_seq(bank.at[s], bank.at[s], bank_send, bank_recv, d).wait_recv()

    @pl.when(reaching & (s < S - 1))
    def _():
        ext(0).wait_recv()
        ext(1).wait_recv()

    for d in range(1, C):
        to_owner(d).wait_recv()
    for b in range(C):
        ctx_ref[:, b * W : (b + 1) * W] = ctx_in[b]
    context = ctx_ref[...]
    width = S * negatives
    mine = lax.rem(lax.broadcasted_iota(jnp.int32, (L, width), 1), K)
    lanes = lax.broadcasted_iota(jnp.int32, (L, 128), 1)
    positives = jnp.zeros((L, 128), jnp.float32)
    negsums = jnp.zeros((L, 128), jnp.float32)
    for j in range(K):
        predicted = dot(context, wpred[j]).astype(jnp.bfloat16)
        begin = pl.multiple_of(c * L + (j + 1) * row_width, row_width)
        products = jnp.zeros((L, CB), jnp.float32)
        logits = jnp.zeros((L, width), jnp.float32)
        for b in range(C):
            part = predicted[:, b * CB : (b + 1) * CB]
            target = feat_all[b, pl.ds(begin, L), :]
            products = products + part.astype(jnp.float32) * target.astype(jnp.float32)
            logits = logits + dot(part, bank[:, b].reshape(width, CB), across)
        positive = jnp.sum(products, axis=1, keepdims=True) * score_scale
        negsum = jnp.sum(
            jnp.where(mine == j, jnp.exp(logits * score_scale), 0.0), axis=1, keepdims=True
        )
        positives = jnp.where(lanes == j, positive, positives)
        negsums = jnp.where(lanes == j, negsum, negsums)
    positives = positives.T[0:8]
    negsums = negsums.T[0:8]
    losses = jnp.log(jnp.exp(positives) + negsums) - positives
    maskf = aux_all[c, MASK_ROW : MASK_ROW + 1, :]
    for j in range(K):
        first = aux_all[c + (j + 1) // 2, MASK_ROW : MASK_ROW + 1, :]
        if (j + 1) % 2:
            second = aux_all[c + (j + 2) // 2, MASK_ROW : MASK_ROW + 1, :]
            first = jnp.concatenate([first[:, row_width:], second[:, :row_width]], axis=1)
        loss_ref[j : j + 1, :] = maskf * first * losses[j : j + 1]

    for copy in sent + tot_copies + bank_copies:
        copy.wait_send()

    @pl.when(reaching & (s > 0))
    def _():
        ext(0).wait_send()
        ext(1).wait_send()

    for d in range(1, S):
        @pl.when(s + d < S)
        def _(d=d):
            state_copy(d).wait_send()
    for d in range(1, C):
        to_owner(d).wait_send()


def shards(S, C, features, w_qkv, log_gate, norm_gain, w_pred, patch_mask, neg_index):
    B, CB = features.shape
    L = B // C
    W = HEADS * HEAD_DIM // C
    inner = HEADS * HEAD_DIM
    vmem = pl.BlockSpec(memory_space=pltpu.VMEM)
    hbm = pl.BlockSpec(memory_space=pl.ANY)
    bf16, f32 = jnp.bfloat16, jnp.float32
    dma = pltpu.SemaphoreType.DMA
    return pl.pallas_call(
        functools.partial(kernel, S, C),
        out_shape=(
            jax.ShapeDtypeStruct((L, inner), bf16),
            jax.ShapeDtypeStruct((K, L), f32),
        ),
        in_specs=[hbm, hbm, vmem, vmem, hbm, vmem, vmem],
        out_specs=(vmem, vmem),
        scratch_shapes=[
            pltpu.VMEM((C, B + 2 * L, CB), bf16),
            pltpu.VMEM((C, 3, CB, W), bf16),
            pltpu.VMEM((C + 2, AUX_ROWS, 128), f32),
            pltpu.VMEM((C, 8, 128), f32),
            pltpu.VMEM((S, 8, 128), f32),
            pltpu.VMEM((S, C, K * C, CB), bf16),
            pltpu.VMEM((3, B, W), f32),
            pltpu.VMEM((3, B, W), bf16),
            pltpu.VMEM((8, B), f32),
            pltpu.VMEM((B, 8), f32),
            pltpu.VMEM((W, HEAD_DIM), bf16),
            pltpu.VMEM((S, W, HEAD_DIM), bf16),
            pltpu.VMEM((W, HEAD_DIM), f32),
            pltpu.VMEM((C, L, W), bf16),
            pltpu.VMEM((C, L, W), bf16),
            pltpu.VMEM(w_pred.shape, bf16),
            dma((5,)),
            dma((C - 1, 5)),
            dma((C - 1, 5)),
            dma((S - 1,)),
            dma((S - 1,)),
            dma((S - 1,)),
            dma((S - 1,)),
            dma((2,)),
            dma((2,)),
            dma((S - 1,)),
            dma((S - 1,)),
            dma((C - 1,)),
            dma((C - 1,)),
        ],
        compiler_params=pltpu.CompilerParams(
            collective_id=0, has_side_effects=True, vmem_limit_bytes=48 * 2**20
        ),
    )(
        features,
        w_qkv,
        log_gate,
        norm_gain.reshape(HEADS, HEAD_DIM),
        w_pred,
        patch_mask.reshape(1, L),
        neg_index,
    )


def solution(mesh):
    placed = (
        P("seq", "ch"),
        P("ch", None),
        P(None, ("seq", "ch")),
        P(),
        P(),
        P(("seq", "ch")),
        P(None, ("seq", "ch")),
    )
    return jax.shard_map(
        functools.partial(shards, mesh.shape["seq"], mesh.shape["ch"]),
        mesh=mesh,
        in_specs=placed,
        out_specs=(P(("seq", "ch"), None), P(None, ("seq", "ch"))),
        check_vma=False,
    )
```

```python
import functools

import jax
import jax.numpy as jnp
from jax import lax
from jax.experimental import pallas as pl
from jax.experimental.pallas import tpu as pltpu
from jax.sharding import PartitionSpec as P

HEADS = 8
HEAD_DIM = 128
K = 4
MASK_ROW = 8
NEG_ROW = 9
AUX_ROWS = 16
MESH = pl.DeviceIdType.MESH
norm_eps = 1e-06
highest = lax.Precision.HIGHEST
across = (((1,), (1,)), ((), ()))
down = (((0,), (0,)), ((), ()))


def dot(a, b, dims=(((1,), (0,)), ((), ())), precision=None):
    return lax.dot_general(a, b, dims, precision=precision, preferred_element_type=jnp.float32)


def split(x):
    high = x.astype(jnp.bfloat16)
    return high, (x - high.astype(jnp.float32)).astype(jnp.bfloat16)


def kernel(
    S, C,
    feat_hbm, w_hbm, gate_hbm, gain_hbm, wpred_hbm, mask_hbm, neg_hbm,
    ctx_ref, loss_ref,
    gate_ref, gain_ref, mask_ref, neg_ref,
    feat_all, w_all, aux_all, sel, totals, bank, proj, qkv, cumrow, cumcol,
    state_out, state_in, carried, ctx_out, ctx_in, wpred,
    small_sem, local_sem, ch_send, ch_recv, feat_send, feat_recv, pass_send, pass_recv,
    w_send, w_recv, share_send, share_recv, tot_send, tot_recv, bank_send, bank_recv,
    ext_send, ext_recv, st_send, st_recv, ctx_send, ctx_recv,
):
    L = gate_ref.shape[1]
    B = C * L
    CB = feat_hbm.shape[1]
    W = qkv.shape[2]
    inner = HEADS * HEAD_DIM
    own_heads = W // HEAD_DIM
    row_width = L // 2
    score_scale = 4.0 * (C * CB) ** (-0.5)
    s, c = lax.axis_index("seq"), lax.axis_index("ch")

    Y = C // 2
    y, core = c // 2, lax.rem(c, 2)
    sibling = c + 1 - 2 * core
    pair = s + 1 - 2 * lax.rem(s, 2)
    half_rows = B // 2
    half_w = CB // 2

    barrier = pltpu.get_barrier_semaphore()
    for d in range(1, C):
        pl.semaphore_signal(
            barrier, inc=1, device_id=(s, lax.rem(c + d, C)), device_id_type=MESH
        )
    for d in range(1, S):
        pl.semaphore_signal(
            barrier, inc=1, device_id=(lax.rem(s + d, S), c), device_id_type=MESH
        )

    small = [
        pltpu.make_async_copy(source, target, small_sem.at[i])
        for i, (source, target) in enumerate(
            ((gate_hbm, gate_ref), (mask_hbm, mask_ref), (neg_hbm, neg_ref), (gain_hbm, gain_ref))
        )
    ]
    own = [pltpu.make_async_copy(feat_hbm, feat_all.at[c, pl.ds(0, B)], local_sem.at[0])]
    for p in range(3):
        begin = pl.multiple_of(p * inner + c * W, 128)
        own.append(
            pltpu.make_async_copy(w_hbm.at[:, pl.ds(begin, W)], w_all.at[c, p], local_sem.at[1 + p])
        )
    for copy in small + own:
        copy.start()
    for copy in small:
        copy.wait()

    aux_all[c, 0:HEADS] = gate_ref[...]
    base = (s * C + c) * L
    local_index = (neg_ref[...] - base).astype(jnp.float32)
    diagonal = lax.broadcasted_iota(jnp.int32, (K, K), 0) == lax.broadcasted_iota(
        jnp.int32, (K, K), 1
    )
    local_index = jnp.sum(
        jnp.where(diagonal, jnp.broadcast_to(local_index, (K, K)), 0.0), axis=1, keepdims=True
    )
    lead = jnp.where(
        lax.broadcasted_iota(jnp.int32, (HEADS, L), 0) == 0,
        jnp.broadcast_to(mask_ref[...].astype(jnp.float32), (HEADS, L)),
        0.0,
    )
    aux_all[c, HEADS:AUX_ROWS] = lead
    aux_all[c, NEG_ROW : NEG_ROW + K] = jnp.broadcast_to(local_index, (K, L))
    pl.semaphore_wait(barrier, S + C - 2)

    def remote(source, target, send, recv, device):
        return pltpu.make_async_remote_copy(
            source, target, send, recv, device_id=device, device_id_type=MESH
        )

    def to_ch(d):
        return remote(
            aux_all.at[c], aux_all.at[c], ch_send.at[d - 1], ch_recv.at[d - 1],
            (s, lax.rem(c + d, C)),
        )

    def columns(p, peer):
        return pl.ds(pl.multiple_of(p * inner + peer * W, 128), W)

    def w_rows(block_s):
        return pl.ds(pl.multiple_of(lax.rem(block_s, 2) * half_w, half_w), half_w)

    def w_to_sibling(p):
        return remote(
            w_hbm.at[:, columns(p, sibling)], w_all.at[c, p],
            w_send.at[0, p], w_recv.at[0, p], (s, sibling),
        )

    def features_to_sibling():
        return remote(
            feat_hbm, feat_all.at[c, pl.ds(0, B)], pass_send.at[0], pass_recv.at[0], (s, sibling)
        )

    def w_across(e, j, p):
        peer = lax.rem(y + e, Y) * 2 + (core + j) % 2
        n = 1 + 2 * (e - 1) + j
        return remote(
            w_hbm.at[w_rows(s), columns(p, peer)], w_all.at[c, p, w_rows(s)],
            w_send.at[n, p], w_recv.at[n, p], (s, peer),
        )

    def features_across(e, j):
        k = (core + j) % 2
        rows = pl.ds(pl.multiple_of(k * half_rows, half_rows), half_rows)
        n = 2 * (e - 1) + j
        return remote(
            feat_hbm.at[rows], feat_all.at[c, rows],
            feat_send.at[n], feat_recv.at[n], (s, lax.rem(y + e, Y) * 2 + k),
        )

    def source(e, j):
        return lax.rem(y + Y - e, Y) * 2 + (core + j) % 2

    def pass_on(e, j, k):
        block = lax.rem(y + Y - e, Y) * 2 + j
        rows = pl.ds(pl.multiple_of(k * half_rows, half_rows), half_rows)
        n = 1 + 2 * (e - 1) + j
        return remote(
            feat_all.at[block, rows], feat_all.at[block, rows],
            pass_send.at[n], pass_recv.at[n], (s, sibling),
        )

    def share(e, j, p, block_s):
        block = source(e, j)
        n = 2 * (e - 1) + j
        return remote(
            w_all.at[block, p, w_rows(block_s)], w_all.at[block, p, w_rows(block_s)],
            share_send.at[n, p], share_recv.at[n, p], (pair, c),
        )

    def to_seq(source, target, sends, recvs, d):
        return remote(
            source, target, sends.at[d - 1], recvs.at[d - 1], (lax.rem(s + d, S), c)
        )

    others = [(e, j) for e in range(1, Y) for j in range(2)]
    sent = [to_ch(d) for d in range(1, C)]
    sent += [w_across(e, j, p) for e, j in others for p in range(3)]
    sent += [features_across(e, j) for e, j in others]
    sent += [features_to_sibling()] + [w_to_sibling(p) for p in range(3)]
    for copy in sent:
        copy.start()
    own_wpred = pltpu.make_async_copy(wpred_hbm, wpred, local_sem.at[4])
    own_wpred.start()
    for d in range(1, C):
        to_ch(d).wait_recv()

    row_id = lax.broadcasted_iota(jnp.int32, (L, L), 0)
    column_id = lax.broadcasted_iota(jnp.int32, (L, L), 1)
    lower = row_id >= column_id
    tril = lower.astype(jnp.float32)
    triu = (row_id <= column_id).astype(jnp.float32)
    sel[...] = jnp.zeros_like(sel)
    row_carry = jnp.zeros((8, 1), jnp.float32)
    column_carry = jnp.zeros((1, 8), jnp.float32)
    for b in range(C):
        for i in range(own_heads):
            sel[b, i : i + 1] = aux_all[b, pl.ds(c * own_heads + i, 1), :]
        gates = sel[b]
        by_row = dot(gates, triu, precision=highest) + row_carry
        by_column = dot(tril, gates, across, precision=highest) + column_carry
        cumrow[:, b * L : (b + 1) * L] = by_row
        cumcol[b * L : (b + 1) * L, :] = by_column
        row_carry = by_row[:, L - 1 : L]
        column_carry = by_column[L - 1 : L, :]
    totals[s] = jnp.broadcast_to(row_carry, (8, 128))
    tot_copies = [to_seq(totals.at[s], totals.at[s], tot_send, tot_recv, d) for d in range(1, S)]
    for copy in tot_copies:
        copy.start()

    def project(block, first=False, last=False):
        for p in range(3):
            part = dot(feat_all[block, 0:B, :], w_all[block, p])
            if not first:
                part = proj[p] + part
            if last:
                qkv[p] = part.astype(jnp.bfloat16)
            else:
                proj[p] = part

    for copy in own:
        copy.wait()
    project(c, first=True)
    for e, j in others:
        for p in range(3):
            w_across(e, j, p).wait_recv()
            copy = share(e, j, p, s)
            copy.start()
            sent.append(copy)
    features_to_sibling().wait_recv()
    for p in range(3):
        w_to_sibling(p).wait_recv()
    project(sibling, last=Y == 1)
    for e, j in others:
        features_across(e, j).wait_recv()
    for e, j in others:
        copy = pass_on(e, j, core)
        copy.start()
        sent.append(copy)
    for e, j in others:
        pass_on(e, j, 1 - core).wait_recv()
    for e, j in others:
        for p in range(3):
            share(e, j, p, pair).wait_recv()
        project(source(e, j), last=(e, j) == others[-1])
    eye = (row_id == column_id).astype(jnp.bfloat16)
    for b in range(C):
        keep = dot(eye, aux_all[b].astype(jnp.bfloat16), across)[:, MASK_ROW : MASK_ROW + 1]
        rows = slice(b * L, (b + 1) * L)
        qkv[2, rows, :] = (qkv[2, rows, :].astype(jnp.float32) * keep).astype(jnp.bfloat16)

    for i in range(own_heads):
        head = slice(i * HEAD_DIM, (i + 1) * HEAD_DIM)
        tail = jnp.exp(cumcol[B - 1 : B, i : i + 1] - cumcol[:, i : i + 1])
        high, low = split(qkv[1, :, head].astype(jnp.float32) * tail)
        values = qkv[2, :, head]
        state_out[head, :] = (dot(high, values, down) + dot(low, values, down)).astype(jnp.bfloat16)

    def state_copy(d):
        return to_seq(state_out, state_in.at[s], st_send, st_recv, d)

    for d in reversed(range(1, S)):
        @pl.when(s + d < S)
        def _(d=d):
            state_copy(d).start()

    wanted = jnp.concatenate([aux_all[b, NEG_ROW : NEG_ROW + K, :] for b in range(C)], axis=0)
    negatives = K * C
    owner = lax.broadcasted_iota(jnp.int32, (negatives, L), 0) // K
    lane = lax.broadcasted_iota(jnp.int32, (negatives, L), 1).astype(jnp.float32)
    hit = wanted == lane
    chosen = jnp.concatenate(
        [jnp.where(hit & (owner == b), 1.0, 0.0) for b in range(C)], axis=1
    ).astype(jnp.bfloat16)
    for b in range(C):
        bank[s, b] = dot(chosen, feat_all[b, 0:B, :]).astype(jnp.bfloat16)
    bank_copies = [to_seq(bank.at[s], bank.at[s], bank_send, bank_recv, d) for d in range(1, S)]
    for copy in bank_copies:
        copy.start()

    def ext(kind, blocks):
        if kind == 0:
            source = feat_all.at[:, pl.ds(0, blocks * L)]
            target = feat_all.at[:, pl.ds(B, blocks * L)]
        else:
            source, target = aux_all.at[pl.ds(0, 2)], aux_all.at[pl.ds(C, 2)]
        return remote(
            source, target, ext_send.at[kind], ext_recv.at[kind], (lax.rem(s + S - 1, S), c)
        )

    def each_ext(condition, act):
        for blocks in (1, 2):
            @pl.when(condition & (c == C - 3 + blocks))
            def _(blocks=blocks):
                for kind in range(2):
                    act(ext(kind, blocks))

    each_ext(s > 0, lambda copy: copy.start())

    @pl.when(s == S - 1)
    def _():
        feat_all[:, B : B + 2 * L, :] = jnp.zeros((C, 2 * L, CB), jnp.bfloat16)
        aux_all[C : C + 2] = jnp.zeros((2, AUX_ROWS, 128), jnp.float32)

    for i in range(own_heads):
        head = slice(i * HEAD_DIM, (i + 1) * HEAD_DIM)
        for b in range(C):
            rows = slice(b * L, (b + 1) * L)
            width = (b + 1) * L
            scores = dot(qkv[0, rows, head], qkv[1, 0:width, head], across)
            diff = cumcol[rows, i : i + 1] - cumrow[i : i + 1, 0:width]
            seen = (
                lax.broadcasted_iota(jnp.int32, (L, width), 0) + b * L
                >= lax.broadcasted_iota(jnp.int32, (L, width), 1)
            )
            decay = jnp.where(seen, jnp.exp(jnp.where(seen, diff, 0.0)), 0.0)
            high, low = split(scores * decay)
            values = qkv[2, 0:width, head]
            proj[0, rows, head] = dot(high, values) + dot(low, values)

    for d in range(1, S):
        to_seq(totals.at[s], totals.at[s], tot_send, tot_recv, d).wait_recv()
    carried[...] = jnp.zeros_like(carried)

    def absorb(turn, _):
        far = s - turn
        pltpu.make_async_remote_copy(
            state_out, state_in.at[turn], st_send.at[far - 1], st_recv.at[far - 1],
            device_id=(lax.rem(s + 1, S), c), device_id_type=MESH,
        ).wait_recv()
        total = totals[turn]
        for i in range(own_heads):
            head = slice(i * HEAD_DIM, (i + 1) * HEAD_DIM)
            carried[head, :] = (
                jnp.exp(total[i : i + 1, :]) * carried[head, :]
                + state_in[turn, head, :].astype(jnp.float32)
            )
        return 0

    lax.fori_loop(0, s, absorb, 0)

    for i in range(own_heads):
        head = slice(i * HEAD_DIM, (i + 1) * HEAD_DIM)
        high, low = split(carried[head, :])
        gain = gain_ref[pl.ds(c * own_heads + i, 1), :]
        for b in range(C):
            rows = slice(b * L, (b + 1) * L)
            queries = qkv[0, rows, head]
            inter = (dot(queries, high) + dot(queries, low)) * jnp.exp(cumcol[rows, i : i + 1])
            mixed = (proj[0, rows, head] + inter) * HEAD_DIM ** (-0.5)
            squares = jnp.mean(mixed * mixed, axis=-1, keepdims=True)
            normed = mixed / jnp.sqrt(squares + norm_eps)
            ctx_out[b, :, head] = (normed * gain).astype(jnp.bfloat16)

    def to_owner(d):
        peer = lax.rem(c + d, C)
        return pltpu.make_async_remote_copy(
            ctx_out.at[peer], ctx_in.at[c], ctx_send.at[d - 1], ctx_recv.at[d - 1],
            device_id=(s, peer), device_id_type=MESH,
        )

    for d in range(1, C):
        to_owner(d).start()
    ctx_in[c] = ctx_out[c]
    own_wpred.wait()
    for d in range(1, S):
        to_seq(bank.at[s], bank.at[s], bank_send, bank_recv, d).wait_recv()

    each_ext(s < S - 1, lambda copy: copy.wait_recv())

    for d in range(1, C):
        to_owner(d).wait_recv()
    for b in range(C):
        ctx_ref[:, b * W : (b + 1) * W] = ctx_in[b]
    context = ctx_ref[...]
    width = S * negatives
    mine = lax.rem(lax.broadcasted_iota(jnp.int32, (L, width), 1), K)
    lanes = lax.broadcasted_iota(jnp.int32, (L, 128), 1)
    positives = jnp.zeros((L, 128), jnp.float32)
    negsums = jnp.zeros((L, 128), jnp.float32)
    for j in range(K):
        predicted = dot(context, wpred[j]).astype(jnp.bfloat16)
        begin = pl.multiple_of(c * L + (j + 1) * row_width, row_width)
        products = jnp.zeros((L, CB), jnp.float32)
        logits = jnp.zeros((L, width), jnp.float32)
        for b in range(C):
            part = predicted[:, b * CB : (b + 1) * CB]
            target = feat_all[b, pl.ds(begin, L), :]
            products = products + part.astype(jnp.float32) * target.astype(jnp.float32)
            logits = logits + dot(part, bank[:, b].reshape(width, CB), across)
        positive = jnp.sum(products, axis=1, keepdims=True) * score_scale
        negsum = jnp.sum(
            jnp.where(mine == j, jnp.exp(logits * score_scale), 0.0), axis=1, keepdims=True
        )
        positives = jnp.where(lanes == j, positive, positives)
        negsums = jnp.where(lanes == j, negsum, negsums)
    positives = positives.T[0:8]
    negsums = negsums.T[0:8]
    losses = jnp.log(jnp.exp(positives) + negsums) - positives
    maskf = aux_all[c, MASK_ROW : MASK_ROW + 1, :]
    for j in range(K):
        first = aux_all[c + (j + 1) // 2, MASK_ROW : MASK_ROW + 1, :]
        if (j + 1) % 2:
            second = aux_all[c + (j + 2) // 2, MASK_ROW : MASK_ROW + 1, :]
            first = jnp.concatenate([first[:, row_width:], second[:, :row_width]], axis=1)
        loss_ref[j : j + 1, :] = maskf * first * losses[j : j + 1]

    for copy in sent + tot_copies + bank_copies:
        copy.wait_send()

    each_ext(s > 0, lambda copy: copy.wait_send())

    for d in range(1, S):
        @pl.when(s + d < S)
        def _(d=d):
            state_copy(d).wait_send()
    for d in range(1, C):
        to_owner(d).wait_send()


def shards(S, C, features, w_qkv, log_gate, norm_gain, w_pred, patch_mask, neg_index):
    B, CB = features.shape
    L = B // C
    W = HEADS * HEAD_DIM // C
    inner = HEADS * HEAD_DIM
    vmem = pl.BlockSpec(memory_space=pltpu.VMEM)
    hbm = pl.BlockSpec(memory_space=pl.ANY)
    bf16, f32 = jnp.bfloat16, jnp.float32
    dma = pltpu.SemaphoreType.DMA
    return pl.pallas_call(
        functools.partial(kernel, S, C),
        out_shape=(
            jax.ShapeDtypeStruct((L, inner), bf16),
            jax.ShapeDtypeStruct((K, L), f32),
        ),
        in_specs=[hbm] * 7,
        out_specs=(vmem, vmem),
        scratch_shapes=[
            pltpu.VMEM((HEADS, L), f32),
            pltpu.VMEM((HEADS, HEAD_DIM), f32),
            pltpu.VMEM((1, L), jnp.int32),
            pltpu.VMEM((1, K), jnp.int32),
            pltpu.VMEM((C, B + 2 * L, CB), bf16),
            pltpu.VMEM((C, 3, CB, W), bf16),
            pltpu.VMEM((C + 2, AUX_ROWS, 128), f32),
            pltpu.VMEM((C, 8, 128), f32),
            pltpu.VMEM((S, 8, 128), f32),
            pltpu.VMEM((S, C, K * C, CB), bf16),
            pltpu.VMEM((3, B, W), f32),
            pltpu.VMEM((3, B, W), bf16),
            pltpu.VMEM((8, B), f32),
            pltpu.VMEM((B, 8), f32),
            pltpu.VMEM((W, HEAD_DIM), bf16),
            pltpu.VMEM((S, W, HEAD_DIM), bf16),
            pltpu.VMEM((W, HEAD_DIM), f32),
            pltpu.VMEM((C, L, W), bf16),
            pltpu.VMEM((C, L, W), bf16),
            pltpu.VMEM(w_pred.shape, bf16),
            dma((4,)),
            dma((5,)),
            dma((C - 1,)),
            dma((C - 1,)),
            dma((C - 2,)),
            dma((C - 2,)),
            dma((C - 1,)),
            dma((C - 1,)),
            dma((C - 1, 3)),
            dma((C - 1, 3)),
            dma((C - 2, 3)),
            dma((C - 2, 3)),
            dma((S - 1,)),
            dma((S - 1,)),
            dma((S - 1,)),
            dma((S - 1,)),
            dma((2,)),
            dma((2,)),
            dma((S - 1,)),
            dma((S - 1,)),
            dma((C - 1,)),
            dma((C - 1,)),
        ],
        compiler_params=pltpu.CompilerParams(
            collective_id=0, has_side_effects=True, vmem_limit_bytes=60 * 2**20
        ),
    )(
        features,
        w_qkv,
        log_gate,
        norm_gain.reshape(HEADS, HEAD_DIM),
        w_pred,
        patch_mask.reshape(1, L),
        neg_index.T,
    )


def solution(mesh):
    placed = (
        P("seq", "ch"),
        P("ch", None),
        P(None, ("seq", "ch")),
        P(),
        P(),
        P(("seq", "ch")),
        P(None, ("seq", "ch")),
    )
    return jax.shard_map(
        functools.partial(shards, mesh.shape["seq"], mesh.shape["ch"]),
        mesh=mesh,
        in_specs=placed,
        out_specs=(P(("seq", "ch"), None), P(None, ("seq", "ch"))),
        check_vma=False,
    )
```

```python
import functools

import jax
import jax.numpy as jnp
from jax import lax
from jax.experimental import pallas as pl
from jax.experimental.pallas import tpu as pltpu
from jax.sharding import PartitionSpec as P

HEADS = 8
HEAD_DIM = 128
K = 4
MASK_ROW = 8
NEG_ROW = 9
AUX_ROWS = 16
MESH = pl.DeviceIdType.MESH
norm_eps = 1e-06
highest = lax.Precision.HIGHEST
across = (((1,), (1,)), ((), ()))
down = (((0,), (0,)), ((), ()))


def dot(a, b, dims=(((1,), (0,)), ((), ())), precision=None):
    return lax.dot_general(a, b, dims, precision=precision, preferred_element_type=jnp.float32)


def split(x):
    high = x.astype(jnp.bfloat16)
    return high, (x - high.astype(jnp.float32)).astype(jnp.bfloat16)


def kernel(
    S, C,
    feat_hbm, w_hbm, gate_hbm, gain_hbm, wpred_hbm, mask_hbm, neg_hbm,
    ctx_ref, loss_ref,
    gate_ref, gain_ref, mask_ref, neg_ref,
    feat_all, w_all, aux_all, sel, totals, bank, proj, qkv, cumrow, cumcol,
    state_out, pair_in, both, halves, gathered, before, carried, ctx_out, ctx_in, wpred,
    small_sem, local_sem, ch_send, ch_recv, feat_send, feat_recv, pass_send, pass_recv,
    w_send, w_recv, share_send, share_recv, tot_send, tot_recv, bank_send, bank_recv,
    ext_send, ext_recv, pair_send, pair_recv, spread_send, spread_recv, st_send, st_recv, ctx_send, ctx_recv,
):
    L = gate_ref.shape[1]
    B = C * L
    CB = feat_hbm.shape[1]
    W = qkv.shape[2]
    inner = HEADS * HEAD_DIM
    own_heads = W // HEAD_DIM
    row_width = L // 2
    score_scale = 4.0 * (C * CB) ** (-0.5)
    s, c = lax.axis_index("seq"), lax.axis_index("ch")

    Y = C // 2
    y, core = c // 2, lax.rem(c, 2)
    sibling = c + 1 - 2 * core
    pair = s + 1 - 2 * lax.rem(s, 2)
    half_rows = B // 2
    half_w = CB // 2

    barrier = pltpu.get_barrier_semaphore()
    for d in range(1, C):
        pl.semaphore_signal(
            barrier, inc=1, device_id=(s, lax.rem(c + d, C)), device_id_type=MESH
        )
    for d in range(1, S):
        pl.semaphore_signal(
            barrier, inc=1, device_id=(lax.rem(s + d, S), c), device_id_type=MESH
        )

    small = [
        pltpu.make_async_copy(source, target, small_sem.at[i])
        for i, (source, target) in enumerate(
            ((gate_hbm, gate_ref), (mask_hbm, mask_ref), (neg_hbm, neg_ref), (gain_hbm, gain_ref))
        )
    ]
    own = [pltpu.make_async_copy(feat_hbm, feat_all.at[c, pl.ds(0, B)], local_sem.at[0])]
    for p in range(3):
        begin = pl.multiple_of(p * inner + c * W, 128)
        own.append(
            pltpu.make_async_copy(w_hbm.at[:, pl.ds(begin, W)], w_all.at[c, p], local_sem.at[1 + p])
        )
    for copy in small + own:
        copy.start()
    for copy in small:
        copy.wait()

    aux_all[c, 0:HEADS] = gate_ref[...]
    base = (s * C + c) * L
    local_index = (neg_ref[...] - base).astype(jnp.float32)
    diagonal = lax.broadcasted_iota(jnp.int32, (K, K), 0) == lax.broadcasted_iota(
        jnp.int32, (K, K), 1
    )
    local_index = jnp.sum(
        jnp.where(diagonal, jnp.broadcast_to(local_index, (K, K)), 0.0), axis=1, keepdims=True
    )
    lead = jnp.where(
        lax.broadcasted_iota(jnp.int32, (HEADS, L), 0) == 0,
        jnp.broadcast_to(mask_ref[...].astype(jnp.float32), (HEADS, L)),
        0.0,
    )
    aux_all[c, HEADS:AUX_ROWS] = lead
    aux_all[c, NEG_ROW : NEG_ROW + K] = jnp.broadcast_to(local_index, (K, L))
    pl.semaphore_wait(barrier, S + C - 2)

    def remote(source, target, send, recv, device):
        return pltpu.make_async_remote_copy(
            source, target, send, recv, device_id=device, device_id_type=MESH
        )

    def to_ch(d):
        return remote(
            aux_all.at[c], aux_all.at[c], ch_send.at[d - 1], ch_recv.at[d - 1],
            (s, lax.rem(c + d, C)),
        )

    def columns(p, peer):
        return pl.ds(pl.multiple_of(p * inner + peer * W, 128), W)

    def w_rows(block_s):
        return pl.ds(pl.multiple_of(lax.rem(block_s, 2) * half_w, half_w), half_w)

    def w_to_sibling(p):
        return remote(
            w_hbm.at[:, columns(p, sibling)], w_all.at[c, p],
            w_send.at[0, p], w_recv.at[0, p], (s, sibling),
        )

    def features_to_sibling():
        return remote(
            feat_hbm, feat_all.at[c, pl.ds(0, B)], pass_send.at[0], pass_recv.at[0], (s, sibling)
        )

    def w_across(e, j, p):
        peer = lax.rem(y + e, Y) * 2 + (core + j) % 2
        n = 1 + 2 * (e - 1) + j
        return remote(
            w_hbm.at[w_rows(s), columns(p, peer)], w_all.at[c, p, w_rows(s)],
            w_send.at[n, p], w_recv.at[n, p], (s, peer),
        )

    def features_across(e, j):
        k = (core + j) % 2
        rows = pl.ds(pl.multiple_of(k * half_rows, half_rows), half_rows)
        n = 2 * (e - 1) + j
        return remote(
            feat_hbm.at[rows], feat_all.at[c, rows],
            feat_send.at[n], feat_recv.at[n], (s, lax.rem(y + e, Y) * 2 + k),
        )

    def source(e, j):
        return lax.rem(y + Y - e, Y) * 2 + (core + j) % 2

    def pass_on(e, j, k):
        block = lax.rem(y + Y - e, Y) * 2 + j
        rows = pl.ds(pl.multiple_of(k * half_rows, half_rows), half_rows)
        n = 1 + 2 * (e - 1) + j
        return remote(
            feat_all.at[block, rows], feat_all.at[block, rows],
            pass_send.at[n], pass_recv.at[n], (s, sibling),
        )

    def share(e, j, p, block_s):
        block = source(e, j)
        n = 2 * (e - 1) + j
        return remote(
            w_all.at[block, p, w_rows(block_s)], w_all.at[block, p, w_rows(block_s)],
            share_send.at[n, p], share_recv.at[n, p], (pair, c),
        )

    def to_seq(source, target, sends, recvs, d):
        return remote(
            source, target, sends.at[d - 1], recvs.at[d - 1], (lax.rem(s + d, S), c)
        )

    others = [(e, j) for e in range(1, Y) for j in range(2)]
    sent = [to_ch(d) for d in range(1, C)]
    sent += [w_across(e, j, p) for e, j in others for p in range(3)]
    sent += [features_across(e, j) for e, j in others]
    sent += [features_to_sibling()] + [w_to_sibling(p) for p in range(3)]
    for copy in sent:
        copy.start()
    own_wpred = pltpu.make_async_copy(wpred_hbm, wpred, local_sem.at[4])
    own_wpred.start()
    for d in range(1, C):
        to_ch(d).wait_recv()

    row_id = lax.broadcasted_iota(jnp.int32, (L, L), 0)
    column_id = lax.broadcasted_iota(jnp.int32, (L, L), 1)
    lower = row_id >= column_id
    tril = lower.astype(jnp.float32)
    triu = (row_id <= column_id).astype(jnp.float32)
    sel[...] = jnp.zeros_like(sel)
    row_carry = jnp.zeros((8, 1), jnp.float32)
    column_carry = jnp.zeros((1, 8), jnp.float32)
    for b in range(C):
        for i in range(own_heads):
            sel[b, i : i + 1] = aux_all[b, pl.ds(c * own_heads + i, 1), :]
        gates = sel[b]
        by_row = dot(gates, triu, precision=highest) + row_carry
        by_column = dot(tril, gates, across, precision=highest) + column_carry
        cumrow[:, b * L : (b + 1) * L] = by_row
        cumcol[b * L : (b + 1) * L, :] = by_column
        row_carry = by_row[:, L - 1 : L]
        column_carry = by_column[L - 1 : L, :]
    totals[s] = jnp.broadcast_to(row_carry, (8, 128))
    tot_copies = [to_seq(totals.at[s], totals.at[s], tot_send, tot_recv, d) for d in range(1, S)]
    for copy in tot_copies:
        copy.start()

    wanted = jnp.concatenate([aux_all[b, NEG_ROW : NEG_ROW + K, :] for b in range(C)], axis=0)
    negatives = K * C
    owner = lax.broadcasted_iota(jnp.int32, (negatives, L), 0) // K
    lane = lax.broadcasted_iota(jnp.int32, (negatives, L), 1).astype(jnp.float32)
    hit = wanted == lane
    chosen = jnp.concatenate(
        [jnp.where(hit & (owner == b), 1.0, 0.0) for b in range(C)], axis=1
    ).astype(jnp.bfloat16)
    own[0].wait()
    bank[c, s] = dot(chosen, feat_all[c, 0:B, :]).astype(jnp.bfloat16)
    bank_copies = [
        to_seq(bank.at[c, s], bank.at[c, s], bank_send, bank_recv, d) for d in range(1, S)
    ]
    for copy in bank_copies:
        copy.start()

    def project(block, first=False, last=False):
        for p in range(3):
            part = dot(feat_all[block, 0:B, :], w_all[block, p])
            if not first:
                part = proj[p] + part
            if last:
                qkv[p] = part.astype(jnp.bfloat16)
            else:
                proj[p] = part

    for copy in own[1:]:
        copy.wait()
    project(c, first=True)
    for e, j in others:
        for p in range(3):
            w_across(e, j, p).wait_recv()
            copy = share(e, j, p, s)
            copy.start()
            sent.append(copy)
    features_to_sibling().wait_recv()
    for p in range(3):
        w_to_sibling(p).wait_recv()
    project(sibling, last=Y == 1)
    for e, j in others:
        features_across(e, j).wait_recv()
    for e, j in others:
        copy = pass_on(e, j, core)
        copy.start()
        sent.append(copy)
    for e, j in others:
        pass_on(e, j, 1 - core).wait_recv()
    for e, j in others:
        for p in range(3):
            share(e, j, p, pair).wait_recv()
        project(source(e, j), last=(e, j) == others[-1])
    eye = (row_id == column_id).astype(jnp.bfloat16)
    for b in range(C):
        keep = dot(eye, aux_all[b].astype(jnp.bfloat16), across)[:, MASK_ROW : MASK_ROW + 1]
        rows = slice(b * L, (b + 1) * L)
        qkv[2, rows, :] = (qkv[2, rows, :].astype(jnp.float32) * keep).astype(jnp.bfloat16)

    for i in range(own_heads):
        head = slice(i * HEAD_DIM, (i + 1) * HEAD_DIM)
        tail = jnp.exp(cumcol[B - 1 : B, i : i + 1] - cumcol[:, i : i + 1])
        high, low = split(qkv[1, :, head].astype(jnp.float32) * tail)
        values = qkv[2, :, head]
        state_out[head, :] = (dot(high, values, down) + dot(low, values, down)).astype(jnp.bfloat16)

    exchange = remote(state_out, pair_in, pair_send.at[0], pair_recv.at[0], (pair, c))
    exchange.start()

    def ext(kind, blocks):
        if kind == 0:
            source = feat_all.at[:, pl.ds(0, blocks * L)]
            target = feat_all.at[:, pl.ds(B, blocks * L)]
        else:
            source, target = aux_all.at[pl.ds(0, 2)], aux_all.at[pl.ds(C, 2)]
        return remote(
            source, target, ext_send.at[kind], ext_recv.at[kind], (lax.rem(s + S - 1, S), c)
        )

    def each_ext(condition, act):
        for blocks in (1, 2):
            @pl.when(condition & (c == C - 3 + blocks))
            def _(blocks=blocks):
                for kind in range(2):
                    act(ext(kind, blocks))

    each_ext(s > 0, lambda copy: copy.start())

    @pl.when(s == S - 1)
    def _():
        feat_all[:, B : B + 2 * L, :] = jnp.zeros((C, 2 * L, CB), jnp.bfloat16)
        aux_all[C : C + 2] = jnp.zeros((2, AUX_ROWS, 128), jnp.float32)

    for d in range(1, S):
        to_seq(totals.at[s], totals.at[s], tot_send, tot_recv, d).wait_recv()
    group, odd = s // 2, lax.rem(s, 2)
    G = S // 2
    half = W // 2
    mine_half = pl.ds(pl.multiple_of(odd * half, half), half)
    other_half = pl.ds(pl.multiple_of((1 - odd) * half, half), half)
    part_rows = min(half, HEAD_DIM)
    exchange.wait_recv()
    is_odd = odd == 1
    for i in range(own_heads):
        head = slice(i * HEAD_DIM, (i + 1) * HEAD_DIM)
        ours = state_out[head, :].astype(jnp.float32)
        theirs = pair_in[head, :].astype(jnp.float32)
        first = jnp.where(is_odd, theirs, ours)
        second = jnp.where(is_odd, ours, theirs)
        later = jnp.exp(totals[2 * group + 1, i : i + 1, :])
        both[head, :] = (later * first + second).astype(jnp.bfloat16)

    def half_copy(d):
        return remote(
            both.at[mine_half], halves.at[group], st_send.at[d - 1], st_recv.at[d - 1],
            (lax.rem(s + 2 * d, S), c),
        )

    for d in reversed(range(1, G)):
        @pl.when(group + d < G)
        def _(d=d):
            half_copy(d).start()

    for d in range(1, S):
        to_seq(bank.at[c, s], bank.at[c, s], bank_send, bank_recv, d).wait_recv()

    def bank_to_ch(d):
        return remote(
            bank.at[c], bank.at[c], spread_send.at[d - 1], spread_recv.at[d - 1],
            (s, lax.rem(c + d, C)),
        )

    for d in range(1, C):
        bank_to_ch(d).start()

    for i in range(own_heads):
        head = slice(i * HEAD_DIM, (i + 1) * HEAD_DIM)
        for b in range(C):
            rows = slice(b * L, (b + 1) * L)
            width = (b + 1) * L
            scores = dot(qkv[0, rows, head], qkv[1, 0:width, head], across)
            diff = cumcol[rows, i : i + 1] - cumrow[i : i + 1, 0:width]
            seen = (
                lax.broadcasted_iota(jnp.int32, (L, width), 0) + b * L
                >= lax.broadcasted_iota(jnp.int32, (L, width), 1)
            )
            decay = jnp.where(seen, jnp.exp(jnp.where(seen, diff, 0.0)), 0.0)
            high, low = split(scores * decay)
            values = qkv[2, 0:width, head]
            proj[0, rows, head] = dot(high, values) + dot(low, values)

    gathered[...] = jnp.zeros_like(gathered)

    def absorb(turn, _):
        far = group - turn
        remote(
            both.at[mine_half], halves.at[turn], st_send.at[far - 1], st_recv.at[far - 1],
            (pair, c),
        ).wait_recv()
        for n in range(half // part_rows):
            rows = slice(n * part_rows, (n + 1) * part_rows)
            h = (odd * half + n * part_rows) // HEAD_DIM
            fade = jnp.exp(
                totals[2 * turn, pl.ds(h, 1), :] + totals[2 * turn + 1, pl.ds(h, 1), :]
            )
            gathered[rows, :] = fade * gathered[rows, :] + halves[turn, rows, :].astype(jnp.float32)
        return 0

    lax.fori_loop(0, group, absorb, 0)
    before[mine_half, :] = gathered[...].astype(jnp.bfloat16)

    swap = remote(
        before.at[mine_half], before.at[mine_half], pair_send.at[1], pair_recv.at[1], (pair, c)
    )
    swapped = remote(
        before.at[other_half], before.at[other_half], pair_send.at[1], pair_recv.at[1], (pair, c)
    )
    swap.start()
    swapped.wait_recv()
    for i in range(own_heads):
        head = slice(i * HEAD_DIM, (i + 1) * HEAD_DIM)
        start = before[head, :].astype(jnp.float32)
        fade = jnp.exp(totals[2 * group, i : i + 1, :])
        carried[head, :] = jnp.where(
            is_odd, fade * start + pair_in[head, :].astype(jnp.float32), start
        )

    for i in range(own_heads):
        head = slice(i * HEAD_DIM, (i + 1) * HEAD_DIM)
        high, low = split(carried[head, :])
        gain = gain_ref[pl.ds(c * own_heads + i, 1), :]
        for b in range(C):
            rows = slice(b * L, (b + 1) * L)
            queries = qkv[0, rows, head]
            inter = (dot(queries, high) + dot(queries, low)) * jnp.exp(cumcol[rows, i : i + 1])
            mixed = (proj[0, rows, head] + inter) * HEAD_DIM ** (-0.5)
            squares = jnp.mean(mixed * mixed, axis=-1, keepdims=True)
            normed = mixed / jnp.sqrt(squares + norm_eps)
            ctx_out[b, :, head] = (normed * gain).astype(jnp.bfloat16)

    def to_owner(d):
        peer = lax.rem(c + d, C)
        return pltpu.make_async_remote_copy(
            ctx_out.at[peer], ctx_in.at[c], ctx_send.at[d - 1], ctx_recv.at[d - 1],
            device_id=(s, peer), device_id_type=MESH,
        )

    for d in range(1, C):
        to_owner(d).start()
    ctx_in[c] = ctx_out[c]
    own_wpred.wait()
    for d in range(1, C):
        bank_to_ch(d).wait_recv()

    each_ext(s < S - 1, lambda copy: copy.wait_recv())

    for d in range(1, C):
        to_owner(d).wait_recv()
    for b in range(C):
        ctx_ref[:, b * W : (b + 1) * W] = ctx_in[b]
    context = ctx_ref[...]
    width = S * negatives
    mine = lax.rem(lax.broadcasted_iota(jnp.int32, (L, width), 1), K)
    lanes = lax.broadcasted_iota(jnp.int32, (L, 128), 1)
    positives = jnp.zeros((L, 128), jnp.float32)
    negsums = jnp.zeros((L, 128), jnp.float32)
    for j in range(K):
        predicted = dot(context, wpred[j]).astype(jnp.bfloat16)
        begin = pl.multiple_of(c * L + (j + 1) * row_width, row_width)
        products = jnp.zeros((L, CB), jnp.float32)
        logits = jnp.zeros((L, width), jnp.float32)
        for b in range(C):
            part = predicted[:, b * CB : (b + 1) * CB]
            target = feat_all[b, pl.ds(begin, L), :]
            products = products + part.astype(jnp.float32) * target.astype(jnp.float32)
            logits = logits + dot(part, bank[b].reshape(width, CB), across)
        positive = jnp.sum(products, axis=1, keepdims=True) * score_scale
        negsum = jnp.sum(
            jnp.where(mine == j, jnp.exp(logits * score_scale), 0.0), axis=1, keepdims=True
        )
        positives = jnp.where(lanes == j, positive, positives)
        negsums = jnp.where(lanes == j, negsum, negsums)
    positives = positives.T[0:8]
    negsums = negsums.T[0:8]
    losses = jnp.log(jnp.exp(positives) + negsums) - positives
    maskf = aux_all[c, MASK_ROW : MASK_ROW + 1, :]
    for j in range(K):
        first = aux_all[c + (j + 1) // 2, MASK_ROW : MASK_ROW + 1, :]
        if (j + 1) % 2:
            second = aux_all[c + (j + 2) // 2, MASK_ROW : MASK_ROW + 1, :]
            first = jnp.concatenate([first[:, row_width:], second[:, :row_width]], axis=1)
        loss_ref[j : j + 1, :] = maskf * first * losses[j : j + 1]

    for copy in sent + tot_copies + bank_copies:
        copy.wait_send()

    each_ext(s > 0, lambda copy: copy.wait_send())

    exchange.wait_send()
    swap.wait_send()
    for d in range(1, G):
        @pl.when(group + d < G)
        def _(d=d):
            half_copy(d).wait_send()
    for d in range(1, C):
        bank_to_ch(d).wait_send()
        to_owner(d).wait_send()


def shards(S, C, features, w_qkv, log_gate, norm_gain, w_pred, patch_mask, neg_index):
    B, CB = features.shape
    L = B // C
    W = HEADS * HEAD_DIM // C
    inner = HEADS * HEAD_DIM
    vmem = pl.BlockSpec(memory_space=pltpu.VMEM)
    hbm = pl.BlockSpec(memory_space=pl.ANY)
    bf16, f32 = jnp.bfloat16, jnp.float32
    dma = pltpu.SemaphoreType.DMA
    return pl.pallas_call(
        functools.partial(kernel, S, C),
        out_shape=(
            jax.ShapeDtypeStruct((L, inner), bf16),
            jax.ShapeDtypeStruct((K, L), f32),
        ),
        in_specs=[hbm] * 7,
        out_specs=(vmem, vmem),
        scratch_shapes=[
            pltpu.VMEM((HEADS, L), f32),
            pltpu.VMEM((HEADS, HEAD_DIM), f32),
            pltpu.VMEM((1, L), jnp.int32),
            pltpu.VMEM((1, K), jnp.int32),
            pltpu.VMEM((C, B + 2 * L, CB), bf16),
            pltpu.VMEM((C, 3, CB, W), bf16),
            pltpu.VMEM((C + 2, AUX_ROWS, 128), f32),
            pltpu.VMEM((C, 8, 128), f32),
            pltpu.VMEM((S, 8, 128), f32),
            pltpu.VMEM((C, S, K * C, CB), bf16),
            pltpu.VMEM((3, B, W), f32),
            pltpu.VMEM((3, B, W), bf16),
            pltpu.VMEM((8, B), f32),
            pltpu.VMEM((B, 8), f32),
            pltpu.VMEM((W, HEAD_DIM), bf16),
            pltpu.VMEM((W, HEAD_DIM), bf16),
            pltpu.VMEM((W, HEAD_DIM), bf16),
            pltpu.VMEM((S // 2, W // 2, HEAD_DIM), bf16),
            pltpu.VMEM((W // 2, HEAD_DIM), f32),
            pltpu.VMEM((W, HEAD_DIM), bf16),
            pltpu.VMEM((W, HEAD_DIM), f32),
            pltpu.VMEM((C, L, W), bf16),
            pltpu.VMEM((C, L, W), bf16),
            pltpu.VMEM(w_pred.shape, bf16),
            dma((4,)),
            dma((5,)),
            dma((C - 1,)),
            dma((C - 1,)),
            dma((C - 2,)),
            dma((C - 2,)),
            dma((C - 1,)),
            dma((C - 1,)),
            dma((C - 1, 3)),
            dma((C - 1, 3)),
            dma((C - 2, 3)),
            dma((C - 2, 3)),
            dma((S - 1,)),
            dma((S - 1,)),
            dma((S - 1,)),
            dma((S - 1,)),
            dma((2,)),
            dma((2,)),
            dma((2,)),
            dma((2,)),
            dma((C - 1,)),
            dma((C - 1,)),
            dma((S // 2 - 1,)),
            dma((S // 2 - 1,)),
            dma((C - 1,)),
            dma((C - 1,)),
        ],
        compiler_params=pltpu.CompilerParams(
            collective_id=0, has_side_effects=True, vmem_limit_bytes=60 * 2**20
        ),
    )(
        features,
        w_qkv,
        log_gate,
        norm_gain.reshape(HEADS, HEAD_DIM),
        w_pred,
        patch_mask.reshape(1, L),
        neg_index.T,
    )


def solution(mesh):
    placed = (
        P("seq", "ch"),
        P("ch", None),
        P(None, ("seq", "ch")),
        P(),
        P(),
        P(("seq", "ch")),
        P(None, ("seq", "ch")),
    )
    return jax.shard_map(
        functools.partial(shards, mesh.shape["seq"], mesh.shape["ch"]),
        mesh=mesh,
        in_specs=placed,
        out_specs=(P(("seq", "ch"), None), P(None, ("seq", "ch"))),
        check_vma=False,
    )
```
